32 devices in a mesh: parts: 2 (over y), blk: 4 (over z), grp: 4 (over x, core).
Axes of the slice: x: 2, y: 2, z: 4, core: 2. Of those that a mesh axis runs over, the one named last changes fastest.
Arguments:
- factors: float32 [64, 4096], P(None, ('parts', 'blk', 'grp')), parts along dimension 1, may hold values from -1 to 1
- tangent: float32 [64, 4096], P(None, ('parts', 'blk', 'grp')), parts along dimension 1, may hold values from -15 to 15
- counts: int32 [4096, 2048], P(('parts', 'blk', 'grp')), parts along dimension 0, may hold values from 0 to 4, as said below
Outputs:
- hess_vec: float32 [64, 4096], P(None, ('parts', 'blk', 'grp')), parts along dimension 1
- residual: float32 [64, 4096], P(None, ('parts', 'blk', 'grp')), parts along dimension 1
- inner: float32 [4], P('parts'), parts along dimension 0
The draws below stay inside these ranges and needn't reach their ends.
There are 2 independent parts, one for each index of `parts`. The reference program is written for one: setup_inputs(seed, part) draws one part's arguments, and reference() takes and returns one part's arrays. A program takes and returns all parts, laid end to end along the dimension named above; each array names one. Nothing has to cross between parts.
Inputs may be any that keep to these rules, and one draw needn't show every extreme that they name: counts is symmetric.
All inputs are finite; a program needn't handle non-finite values.
Results may differ from the reference program's by a relative error of at most 0.0003.
Values sent between devices are 32-bit elements; how exact they have to be, the bound alone decides.
No kernel may reach another device: no remote copies, remote signals or barrier semaphores. Data moves between devices by JAX's collectives and lax.ppermute only.
A program may use at most 128 MiB of HBM per device.

```python
import jax
import jax.numpy as jnp
from jax import lax

RANK = 64
ROWS_DEV = 128
NODES = 2048
N_BLK = 4
N_GRP = 4


def draw_tangent(key, part):
    key_base = jax.random.fold_in(key, 11)
    key_jit = jax.random.fold_in(key, 12)
    node = jnp.arange(NODES, dtype=jnp.float32) / NODES
    jitter = jnp.exp(jax.random.uniform(key_jit, (1, NODES), jnp.float32, jnp.log(0.6), jnp.log(1.6)))
    base = jnp.clip(jax.random.normal(key_base, (RANK, NODES), jnp.float32), -4.0, 4.0)
    rise = jnp.exp(jnp.log(3.0) * node)[None, :]
    return 0.25 * base * rise * jitter


def draw_counts(key, part):
    upper = jax.random.randint(jax.random.fold_in(key, 21), (NODES, NODES), 0, 3, dtype=jnp.int32)
    return upper + upper.T


def block_levels(own_key, dims, shards, smallest, high):
    level, own = 1.0, jax.random.fold_in(own_key, 6)
    for dim, blocks in shards:
        steps = jnp.exp(jax.random.uniform(jax.random.fold_in(own, dim), (blocks,), jnp.float32, smallest / len(shards), high / len(shards)))
        level = level * jnp.repeat(steps, dims[dim] // blocks).reshape([-1 if axis == dim else 1 for axis in range(len(dims))])
    return level


def scatter_about(rng, shape, width, bound, cuts=(), kind=jnp.bfloat16):
    drawn = jax.random.normal(rng, shape, jnp.float32) * width
    if len(cuts) > 0:
        drawn = block_levels(rng, shape, cuts, -0.22, 0.18) * drawn
    return jnp.clip(drawn, min=-bound, max=bound).astype(kind)


def setup_inputs(seed: int = 0, part: int = 0) -> dict:
    keys = jax.random.split(jax.random.key(seed), 4)
    own_keys = jax.random.split(jax.random.fold_in(keys[3], part), 4)
    return {
        "factors": scatter_about(own_keys[0], (RANK, NODES), 0.25, 1.0, ((1, 16),), jnp.float32),
        "tangent": draw_tangent(jax.random.fold_in(jax.random.fold_in(keys[3], part), 71), part),
        "counts": draw_counts(jax.random.fold_in(jax.random.fold_in(keys[3], part), 71), part),
    }


def reference(factors, tangent, counts):
    scale = 1.0 / jnp.sqrt(jnp.float32(NODES))
    step = ROWS_DEV * N_GRP
    highest = lax.Precision.HIGHEST
    contract = (((0,), (0,)), ((), ()))
    right = (((1,), (1,)), ((), ()))

    def one_block(index):
        start = (index * step).astype(jnp.int32)
        row_u = lax.dynamic_slice_in_dim(factors, start, step, 1)
        row_v = lax.dynamic_slice_in_dim(tangent, start, step, 1)
        row_c = lax.dynamic_slice_in_dim(counts, start, step, 0).astype(jnp.float32)
        eta = lax.dot_general(row_u, factors, contract, precision=highest)
        deta = lax.dot_general(row_u, tangent, contract, precision=highest) + lax.dot_general(row_v, factors, contract, precision=highest)
        row_ids = start + jnp.arange(step, dtype=jnp.int32)[:, None]
        col_ids = jnp.arange(NODES, dtype=jnp.int32)[None, :]
        keep = row_ids != col_ids
        rate = jnp.where(keep, jnp.exp(eta), jnp.float32(0.0))
        weight = rate * deta
        slack = jnp.where(keep, row_c - rate, jnp.float32(0.0))
        hess_part = lax.dot_general(factors, weight, right, precision=highest)
        resid_part = lax.dot_general(factors, slack - weight, right, precision=highest)
        return (hess_part, resid_part)
    hess_blocks, resid_blocks = lax.map(one_block, jnp.arange(N_BLK, dtype=jnp.int32))
    hess_vec = jnp.transpose(hess_blocks, (1, 0, 2)).reshape(RANK, NODES) * scale
    residual = jnp.transpose(resid_blocks, (1, 0, 2)).reshape(RANK, NODES) * scale
    inner = jnp.stack([jnp.sum(residual * residual), jnp.sum(tangent * hess_vec)])
    return (hess_vec, residual, inner)
```

```python
import functools

import jax
import jax.numpy as jnp
from jax import lax
from jax.experimental import pallas as pl
from jax.experimental.pallas import tpu as pltpu
from jax.sharding import PartitionSpec as P

AXES = ("blk", "grp")
F32, BF16 = jnp.float32, jnp.bfloat16


def source(index, step, size):
    if size & (size - 1) == 0:
        return index ^ step
    return (index + size - step) % size


def exchange(x, blks, grps, step_blk, step_x, step_core):
    cores = 2 if grps % 2 == 0 else 1
    chips = grps // cores
    pairs = []
    for b in range(blks):
        for g in range(grps):
            sb = source(b, step_blk, blks)
            sx = source(g // cores, step_x, chips)
            sc = source(g % cores, step_core, cores)
            pairs.append(((sb * chips + sx) * cores + sc, b * grps + g))
    return lax.ppermute(x, AXES, pairs)


def split2(x):
    hi = x.astype(BF16)
    return hi, (x - hi.astype(F32)).astype(BF16)


def split3(x):
    hi = x.astype(BF16)
    rest = x - hi.astype(F32)
    mid = rest.astype(BF16)
    return hi, mid, (rest - mid.astype(F32)).astype(BF16)


def dot(a, b):
    return lax.dot_general(a, b, (((1,), (0,)), ((), ())), preferred_element_type=F32)


def dot_t(a, b):
    return lax.dot_general(a, b, (((1,), (1,)), ((), ())), preferred_element_type=F32)


def left_operands(own, rank):
    rows = own.T
    uh, um, ul = split3(rows[:, :rank])
    vh, vm = split2(rows[:, rank:])
    none = jnp.zeros_like(uh)
    first = jnp.concatenate(
        [jnp.concatenate([uh, uh, none, none], 1), jnp.concatenate([vh, vh, uh, uh], 1)], 0
    )
    second = jnp.concatenate(
        [jnp.concatenate([um, um, none, none], 1), jnp.concatenate([vm, vm, um, um], 1)], 0
    )
    third = jnp.concatenate([ul, none, none, none], 1)
    return first, second, third, uh


def tile_terms(left, cols, tile_counts, rank, diagonal):
    first, second, third, uh_rows = left
    rows = third.shape[0]
    uh, um, ul = split3(cols[:rank])
    vh, vm = split2(cols[rank:])
    right = jnp.concatenate([uh, um, vh, vm], 0)
    both = dot(first, right) + dot(second, right)
    eta = both[:rows] + (dot(third, right) + dot(uh_rows, ul))
    deta = both[rows:]
    rate = jnp.exp(eta)
    counted = tile_counts.astype(F32)
    if diagonal:
        keep = lax.broadcasted_iota(jnp.int32, rate.shape, 0) != lax.broadcasted_iota(
            jnp.int32, rate.shape, 1
        )
        rate = jnp.where(keep, rate, 0.0)
        counted = jnp.where(keep, counted, 0.0)
    weight = rate * deta
    wh, wm = split2(weight)
    sh, sm = split2(counted - rate - weight)
    out = dot_t(jnp.concatenate([uh, um], 0), jnp.concatenate([wh, sh, wm, sm], 0))
    total = out[:rank] + out[rank:]
    total = total[:, : 2 * rows] + total[:, 2 * rows :]
    return total


def columns_of(counts_ref, place, rows):
    return counts_ref[:, pl.ds(pl.multiple_of(place * rows, rows), rows)]


def own_kernel(rank, places, *refs):
    blocks, counts_ref, out_ref = refs[:-2], refs[-2], refs[-1]
    rows = counts_ref.shape[0]
    spots = places()
    left = left_operands(blocks[0][...], rank)
    total = None
    for at in range(0, len(blocks), 2):
        group = range(at, min(at + 2, len(blocks)))
        cols = jnp.concatenate([blocks[k][...] for k in group], 1)
        tile = jnp.concatenate([columns_of(counts_ref, spots[k], rows) for k in group], 1)
        part = tile_terms(left, cols, tile, rank, at == 0)
        total = part if total is None else total + part
    out_ref[...] = total


def last_kernel(rank, places, scale, own_ref, other_ref, counts_ref, sum_ref, hess_ref, resid_ref, inner_ref):
    rows = counts_ref.shape[0]
    spots = places()
    own = own_ref[...]
    left = left_operands(own, rank)
    total = sum_ref[...]
    for at in range(0, other_ref.shape[0], 2):
        group = range(at, min(at + 2, other_ref.shape[0]))
        cols = jnp.concatenate([other_ref[k] for k in group], 1)
        tile = jnp.concatenate([columns_of(counts_ref, spots[k], rows) for k in group], 1)
        total = total + tile_terms(left, cols, tile, rank, False)
    hess = total[:, :rows] * scale
    resid = total[:, rows:] * scale
    hess_ref[...] = hess
    resid_ref[...] = resid
    sum_sq = jnp.sum(resid * resid)
    sum_curv = jnp.sum(own[rank:] * hess)
    lane = lax.broadcasted_iota(jnp.int32, inner_ref.shape, 1)
    inner_ref[...] = jnp.where(lane == 0, sum_sq, jnp.where(lane == 1, sum_curv, 0.0))


def local(factors, tangent, counts):
    rank, rows = factors.shape
    nodes = counts.shape[1]
    blks, grps = lax.axis_size("blk"), lax.axis_size("grp")
    cores = 2 if grps % 2 == 0 else 1
    chips = grps // cores
    swap = functools.partial(exchange, blks=blks, grps=grps)

    own = jnp.concatenate([factors, tangent], 0)
    steps = [(b, x) for x in range(chips) for b in range(blks)]
    blocks = {(0, 0): own}
    for b in reversed(range(1, blks)):
        blocks[b, 0] = swap(own, step_blk=b, step_x=0, step_core=0)
    for x in range(1, chips):
        for b in range(blks):
            blocks[b, x] = swap(blocks[b, 0], step_blk=0, step_x=x, step_core=0)
    blocks = [blocks[step] for step in steps]

    def places(core_step):
        b, g = lax.axis_index("blk"), lax.axis_index("grp")
        x, c = g // cores, g % cores
        return [
            (source(b, sb, blks) * chips + source(x, sx, chips)) * cores
            + source(c, core_step, cores)
            for sb, sx in steps
        ]

    vmem = pl.BlockSpec(memory_space=pltpu.VMEM)
    params = pltpu.CompilerParams(vmem_limit_bytes=40 * 1024 * 1024)
    total = pl.pallas_call(
        functools.partial(own_kernel, rank, lambda: places(0)),
        out_shape=jax.ShapeDtypeStruct((rank, 2 * rows), F32),
        in_specs=[vmem] * (len(blocks) + 1),
        out_specs=vmem,
        compiler_params=params,
        name="own_core_blocks",
    )(*blocks, counts)
    others = (
        swap(jnp.stack(blocks), step_blk=0, step_x=0, step_core=1)
        if cores == 2
        else jnp.zeros((0, 2 * rank, rows), F32)
    )
    hess_vec, residual, inner = pl.pallas_call(
        functools.partial(last_kernel, rank, lambda: places(1), 1.0 / nodes**0.5),
        out_shape=(
            jax.ShapeDtypeStruct((rank, rows), F32),
            jax.ShapeDtypeStruct((rank, rows), F32),
            jax.ShapeDtypeStruct((1, 128), F32),
        ),
        in_specs=[vmem] * 4,
        out_specs=(vmem, vmem, vmem),
        compiler_params=params,
        name="other_core_blocks",
    )(own, others, counts, total)

    for x in range(1):
        terms = [
            swap(inner, step_blk=0, step_x=sx, step_core=sc)
            for sx in range(chips)
            for sc in range(cores)
            if (sx, sc) != (0, 0)
        ]
        inner = sum(terms, inner)
        terms = [swap(inner, step_blk=sb, step_x=0, step_core=0) for sb in range(1, blks)]
        inner = sum(terms, inner)
    return hess_vec, residual, inner[0, :2]


def solution(mesh):
    part = ("parts", "blk", "grp")
    return jax.shard_map(
        local,
        mesh=mesh,
        in_specs=(P(None, part), P(None, part), P(part, None)),
        out_specs=(P(None, part), P(None, part), P("parts")),
        check_vma=False,
    )
```

```python
import functools

import jax
import jax.numpy as jnp
from jax import lax
from jax.experimental import pallas as pl
from jax.experimental.pallas import tpu as pltpu
from jax.sharding import PartitionSpec as P

AXES = ("blk", "grp")
CORES = 2
FAR, NEAR = 1, 0
F32, BF16 = jnp.float32, jnp.bfloat16


def permute(x, blks, chips, moves):
    pairs = []
    for b in range(blks):
        for x_at in range(chips):
            for c in range(CORES):
                step = moves[c]
                to = ((b ^ step[0]) * chips + (x_at ^ step[1])) * CORES + (c ^ step[2])
                pairs.append(((b * chips + x_at) * CORES + c, to))
    return lax.ppermute(x, AXES, pairs)


def split2(x):
    hi = x.astype(BF16)
    return hi, (x - hi.astype(F32)).astype(BF16)


def split3(x):
    hi = x.astype(BF16)
    rest = x - hi.astype(F32)
    mid = rest.astype(BF16)
    return hi, mid, (rest - mid.astype(F32)).astype(BF16)


def dot(a, b):
    return lax.dot_general(a, b, (((1,), (0,)), ((), ())), preferred_element_type=F32)


def dot_t(a, b):
    return lax.dot_general(a, b, (((1,), (1,)), ((), ())), preferred_element_type=F32)


def schedule(blks, chips):
    half = blks // 2
    if (blks, chips) == (4, 2):
        ops = [
            (None, (3, 0, 0), (0, 1, 0)),
            (None, (2, 0, 0), (1, 0, 0)),
            (0, (0, 1, 0), (1, 0, 0)),
            (1, (0, 1, 1), (0, 0, 1)),
        ]
        return ops, [(0, 0), (1, 1), (2, 2), (None, 3)], [[0, 1], [2], [3]]
    ops, slots = [], []
    far = [(b, x) for x in range(chips) for b in range(half, blks)]
    near = [(b, x) for x in range(chips) for b in range(half)][1:] + far[-1:]
    for k in range(len(far)):
        src = k % half if k >= half else None
        (fb, fx), (nb, nx) = (far[src], near[src]) if k >= half else ((0, 0), (0, 0))
        far_move = (far[k][0] ^ fb, far[k][1] ^ fx, 0)
        near_move = (near[k][0] ^ nb, near[k][1] ^ nx, 0)
        if k == len(far) - 1:
            far_move, near_move = (*far_move[:2], 1), (0, 0, 1)
        ops.append((src, far_move, near_move))
        slots.append((k, k))
    slots[-1] = (None, len(far) - 1)
    return ops, slots, [range(half), range(half, len(far) - 1), [len(far) - 1]]


def left_kernel(rank, chip_ref, counts_ref, other_counts_ref, first_ref, second_ref, third_ref):
    span = 2 * rank
    nodes = jnp.concatenate([chip_ref[:span].T, chip_ref[span:].T], 0)
    uh, um, ul = split3(nodes[:, :rank])
    vh, vm = split2(nodes[:, rank:])
    none = jnp.zeros_like(uh)
    first_ref[...] = jnp.concatenate(
        [jnp.concatenate([uh, uh, none, none], 1), jnp.concatenate([vh, vh, uh, uh], 1)], 0
    )
    second_ref[...] = jnp.concatenate(
        [jnp.concatenate([um, um, none, none], 1), jnp.concatenate([vm, vm, um, um], 1)], 0
    )
    third_ref[...] = jnp.concatenate([ul, uh], 1)


def chip_terms(left, chip, tile_counts, rank, diagonal):
    first, second, third = left
    rows = third.shape[0]
    span = 2 * rank
    cols = jnp.concatenate([chip[:span], chip[span:]], 1)
    uh, um, ul = split3(cols[:rank])
    vh, vm = split2(cols[rank:])
    right = jnp.concatenate([uh, um, vh, vm], 0)
    eta = dot(
        jnp.concatenate([first[:rows], second[:rows], third], 1),
        jnp.concatenate([right, right, uh, ul], 0),
    )
    deta = dot(
        jnp.concatenate([first[rows:], second[rows:]], 1), jnp.concatenate([right, right], 0)
    )
    rate = jnp.exp(eta)
    counted = tile_counts.astype(F32)
    if diagonal is not None:
        at_row = lax.broadcasted_iota(jnp.int32, rate.shape, 0)
        at_col = lax.broadcasted_iota(jnp.int32, rate.shape, 1)
        keep = jnp.logical_or(at_row != at_col, jnp.logical_not(diagonal))
        rate = jnp.where(keep, rate, 0.0)
        counted = jnp.where(keep, counted, 0.0)
    weight = rate * deta
    wh, wm = split2(weight)
    sh, sm = split2(counted - rate - weight)
    out = dot_t(jnp.concatenate([uh, um], 0), jnp.concatenate([wh, sh, wm, sm], 0))
    total = out[:rank] + out[rank:]
    return total[:, : 2 * rows] + total[:, 2 * rows :]


def tile_of(counts_ref, other_counts_ref, place):
    rows = counts_ref.shape[0]
    chip, me = place
    lines = []
    for ref in (counts_ref, other_counts_ref):
        halves = [
            ref[:, pl.ds(pl.multiple_of((chip * CORES + half) * rows, rows), rows)]
            for half in (me, 1 - me)
        ]
        lines.append(jnp.concatenate(halves, 1))
    return jnp.concatenate(lines, 0)


def chips_kernel(rank, places, is_far, plan, part, *refs):
    left = [ref[...] for ref in refs[:3]]
    counts_ref, other_ref = refs[3:5]
    count = 1 + max(max(entry[:2]) for entry in plan)
    blocks = refs[5 : 5 + count]
    rest = refs[5 + count :]
    rows = counts_ref.shape[0]
    outs = 2 if part else 1
    total = rest[0][...] if len(rest) > outs else None
    far = is_far()
    for (at_far, at_near, is_own), place in zip(plan, places()):
        chip = blocks[at_far][...]
        if at_far != at_near:
            chip = jnp.where(far, chip, blocks[at_near][...])
        tile = tile_of(counts_ref, other_ref, place)
        own_core = {FAR: far, NEAR: jnp.logical_not(far), None: None}[is_own]
        terms = chip_terms(left, chip, tile, rank, own_core)
        total = terms if total is None else total + terms
    if part:
        mine_ref, theirs_ref = rest[-2:]
        mine_ref[...] = jnp.concatenate([total[:, :rows], total[:, 2 * rows : 3 * rows]], 1)
        theirs_ref[...] = jnp.concatenate([total[:, rows : 2 * rows], total[:, 3 * rows :]], 1)
    else:
        rest[-1][...] = total


def finish_kernel(rank, scale, tangent_ref, mine_ref, got_ref, hess_ref, resid_ref, inner_ref):
    rows = tangent_ref.shape[1]
    total = (mine_ref[...] + got_ref[...]) * scale
    hess, resid = total[:, :rows], total[:, rows:]
    hess_ref[...] = hess
    resid_ref[...] = resid
    sum_sq = jnp.sum(resid * resid)
    sum_curv = jnp.sum(tangent_ref[rank:] * hess)
    lane = lax.broadcasted_iota(jnp.int32, inner_ref.shape, 1)
    inner_ref[...] = jnp.where(lane == 0, sum_sq, jnp.where(lane == 1, sum_curv, 0.0))


def local(factors, tangent, counts):
    rank, rows = factors.shape
    nodes = counts.shape[1]
    blks, grps = lax.axis_size("blk"), lax.axis_size("grp")
    chips = grps // CORES
    def is_far():
        return lax.axis_index("grp") % CORES == FAR

    vmem = pl.BlockSpec(memory_space=pltpu.VMEM)
    params = pltpu.CompilerParams(vmem_limit_bytes=40 * 1024 * 1024)

    def call(kernel, name, out_shape, *args):
        return pl.pallas_call(
            kernel,
            out_shape=out_shape,
            in_specs=[vmem] * len(args),
            out_specs=jax.tree.map(lambda _: vmem, out_shape),
            compiler_params=params,
            name=name,
        )(*args)

    def shape(*dims, dtype=F32):
        return jax.ShapeDtypeStruct(dims, dtype)

    swap_cores = functools.partial(permute, blks=blks, chips=chips, moves=[(0, 0, 1)] * 2)
    own = lax.optimization_barrier(jnp.concatenate([factors, tangent], 0))
    chip = jnp.concatenate([own, swap_cores(factors), swap_cores(tangent)], 0)
    (chip, counts) = lax.optimization_barrier((chip, counts))
    other_counts = swap_cores(counts)

    ops, slots, groups = schedule(blks, chips)
    left = call(
        functools.partial(left_kernel, rank),
        "row_operands",
        tuple(
            shape(n * rows, k * rank, dtype=BF16) for n, k in ((4, 4), (4, 4), (2, 2))
        ),
        chip,
        counts,
        other_counts,
    )
    got, holds = {None: chip}, {None: {FAR: (0, 0, FAR), NEAR: (0, 0, NEAR)}}
    for k, (src, far_move, near_move) in enumerate(ops):
        if k == 2:
            (left, got[src]) = lax.optimization_barrier((left, got[src]))
        sent = {FAR: far_move, NEAR: near_move}
        got[k] = permute(got[src], blks, chips, [sent[core] for core in range(CORES)])
        holds[k] = {}
        for core in (FAR, NEAR):
            sender = core ^ sent[core][2]
            b, x, first = holds[src][sender]
            holds[k][core] = (b ^ sent[sender][0], x ^ sent[sender][1], first)

    def places(entries):
        b, g = lax.axis_index("blk"), lax.axis_index("grp")
        far, x = is_far(), g // CORES
        found = []
        for at_far, at_near in entries:
            ours, theirs = holds[at_far][FAR], holds[at_near][NEAR]
            step_b, step_x, first = (jnp.where(far, p, q) for p, q in zip(ours, theirs))
            found.append(((b ^ step_b) * chips + (x ^ step_x), first))
        return found

    total = ()
    for group in groups:
        entries = [slots[k] for k in group]
        used = []
        for entry in entries:
            used += [k for k in dict.fromkeys(entry) if k not in used]
        plan = [
            (used.index(p), used.index(q), FAR if p is None else NEAR if q is None else None)
            for p, q in entries
        ]
        part = group is groups[-1]
        total = call(
            functools.partial(
                chips_kernel, rank, functools.partial(places, entries), is_far, plan, part
            ),
            "chips_" + "_".join(map(str, group)),
            (shape(rank, 2 * rows),) * 2 if part else (shape(rank, 4 * rows),),
            *left,
            counts,
            other_counts,
            *[got[k] for k in used],
            *total,
        )
    mine, theirs = total
    hess_vec, residual, inner = call(
        functools.partial(finish_kernel, rank, 1.0 / nodes**0.5),
        "finish",
        (shape(rank, rows), shape(rank, rows), shape(1, 128)),
        own,
        mine,
        swap_cores(theirs),
    )
    size = blks * grps
    spread = jnp.broadcast_to(inner[None], (size, 1, 128))
    order = [list(range(size))[::-1]]
    inner = lax.all_to_all(spread, AXES, 0, 0, axis_index_groups=order, tiled=True).sum(0)
    return hess_vec, residual, inner[0, :2]


def solution(mesh):
    part = ("parts", "blk", "grp")
    return jax.shard_map(
        local,
        mesh=mesh,
        in_specs=(P(None, part), P(None, part), P(part, None)),
        out_specs=(P(None, part), P(None, part), P("parts")),
        check_vma=False,
    )
```

```python
import functools

import jax
import jax.numpy as jnp
from jax import lax
from jax.experimental import pallas as pl
from jax.experimental.pallas import tpu as pltpu
from jax.sharding import PartitionSpec as P

AXES = ("blk", "grp")
CORES = 2
FAR, NEAR = 1, 0
F32, BF16 = jnp.float32, jnp.bfloat16


def permute(x, blks, chips, moves):
    pairs = []
    for b in range(blks):
        for x_at in range(chips):
            for c in range(CORES):
                step = moves[c]
                to = ((b ^ step[0]) * chips + (x_at ^ step[1])) * CORES + (c ^ step[2])
                pairs.append(((b * chips + x_at) * CORES + c, to))
    return lax.ppermute(x, AXES, pairs)


def split2(x):
    hi = x.astype(BF16)
    return hi, (x - hi.astype(F32)).astype(BF16)


def split3(x):
    hi = x.astype(BF16)
    rest = x - hi.astype(F32)
    mid = rest.astype(BF16)
    return hi, mid, (rest - mid.astype(F32)).astype(BF16)


def dot(a, b):
    return lax.dot_general(a, b, (((1,), (0,)), ((), ())), preferred_element_type=F32)


def dot_t(a, b):
    return lax.dot_general(a, b, (((1,), (1,)), ((), ())), preferred_element_type=F32)


def schedule(blks, chips):
    half = blks // 2
    if (blks, chips) == (4, 2):
        ops = [
            (None, (2, 0, 0), (0, 1, 0)),
            (None, (3, 1, 1), (1, 0, 1)),
            (0, (1, 0, 1), (0, 0, 1)),
            (0, (0, 1, 1), (1, 0, 1)),
        ]
        return ops, [(None, 0), (0, 1), (1, 2), (3, 3)], [[0], [1], [2], [3]]
    ops, slots = [], []
    far = [(b, x) for x in range(chips) for b in range(half, blks)]
    near = [(b, x) for x in range(chips) for b in range(half)][1:] + far[-1:]
    for k in range(len(far)):
        src = k % half if k >= half else None
        (fb, fx), (nb, nx) = (far[src], near[src]) if k >= half else ((0, 0), (0, 0))
        far_move = (far[k][0] ^ fb, far[k][1] ^ fx, 0)
        near_move = (near[k][0] ^ nb, near[k][1] ^ nx, 0)
        if k == len(far) - 1:
            far_move, near_move = (*far_move[:2], 1), (0, 0, 1)
        ops.append((src, far_move, near_move))
        slots.append((k, k))
    slots[-1] = (None, len(far) - 1)
    return ops, slots, [range(half), range(half, len(far) - 1), [len(far) - 1]]


def left_kernel(
    rank, places, chip_ref, counts_ref, other_ref, first_ref, second_ref, third_ref, tiles_ref
):
    span = 2 * rank
    nodes = jnp.concatenate([chip_ref[:span].T, chip_ref[span:].T], 0)
    uh, um, ul = split3(nodes[:, :rank])
    vh, vm = split2(nodes[:, rank:])
    none = jnp.zeros_like(uh)
    first_ref[...] = jnp.concatenate(
        [jnp.concatenate([uh, uh, none, none], 1), jnp.concatenate([vh, vh, uh, uh], 1)], 0
    )
    second_ref[...] = jnp.concatenate(
        [jnp.concatenate([um, um, none, none], 1), jnp.concatenate([vm, vm, um, um], 1)], 0
    )
    third_ref[...] = jnp.concatenate([ul, uh], 1)
    for k, place in enumerate(places()):
        tiles_ref[k] = tile_of(counts_ref, other_ref, place).astype(F32)


def chip_terms(left, chip, counted, rank, diagonal):
    first, second, third = left
    rows = third.shape[0]
    span = 2 * rank
    cols = jnp.concatenate([chip[:span], chip[span:]], 1)
    uh, um, ul = split3(cols[:rank])
    vh, vm = split2(cols[rank:])
    right = jnp.concatenate([uh, um, vh, vm], 0)
    eta = dot(
        jnp.concatenate([first[:rows], second[:rows], third], 1),
        jnp.concatenate([right, right, uh, ul], 0),
    )
    deta = dot(
        jnp.concatenate([first[rows:], second[rows:]], 1), jnp.concatenate([right, right], 0)
    )
    rate = jnp.exp(eta)
    if diagonal is not None:
        at_row = lax.broadcasted_iota(jnp.int32, rate.shape, 0)
        at_col = lax.broadcasted_iota(jnp.int32, rate.shape, 1)
        keep = jnp.logical_or(at_row != at_col, jnp.logical_not(diagonal))
        rate = jnp.where(keep, rate, 0.0)
        counted = jnp.where(keep, counted, 0.0)
    weight = rate * deta
    wh, wm = split2(weight)
    sh, sm = split2(counted - rate - weight)
    out = dot_t(jnp.concatenate([uh, um], 0), jnp.concatenate([wh, sh, wm, sm], 0))
    total = out[:rank] + out[rank:]
    return total[:, : 2 * rows] + total[:, 2 * rows :]


def tile_of(counts_ref, other_counts_ref, place):
    rows = counts_ref.shape[0]
    chip, first = place
    lines = []
    for ref in (counts_ref, other_counts_ref):
        halves = [
            ref[:, pl.ds(pl.multiple_of((chip * CORES + half) * rows, rows), rows)]
            for half in (first, 1 - first)
        ]
        lines.append(jnp.concatenate(halves, 1))
    return jnp.concatenate(lines, 0)


def chips_kernel(rank, is_far, plan, part, slot, *refs):
    left = [ref[...] for ref in refs[:3]]
    tiles_ref = refs[3]
    count = 1 + max(max(entry[:2]) for entry in plan)
    blocks = refs[4 : 4 + count]
    rest = refs[4 + count :]
    rows = tiles_ref.shape[1] // CORES
    outs = 2 if part else 1
    total = rest[0][...] if len(rest) > outs else None
    far = is_far()
    for k, (at_far, at_near, is_own) in enumerate(plan):
        chip = blocks[at_far][...]
        if at_far != at_near:
            chip = jnp.where(far, chip, blocks[at_near][...])
        own_core = {FAR: far, NEAR: jnp.logical_not(far), None: None}[is_own]
        terms = chip_terms(left, chip, tiles_ref[slot + k], rank, own_core)
        total = terms if total is None else total + terms
    if part:
        mine_ref, theirs_ref = rest[-2:]
        mine_ref[...] = jnp.concatenate([total[:, :rows], total[:, 2 * rows : 3 * rows]], 1)
        theirs_ref[...] = jnp.concatenate([total[:, rows : 2 * rows], total[:, 3 * rows :]], 1)
    else:
        rest[-1][...] = total


def finish_kernel(rank, scale, own_ref, mine_ref, got_ref, total_ref, inner_ref):
    rows = own_ref.shape[1]
    total = (mine_ref[...] + got_ref[...]) * scale
    total_ref[...] = total
    hess, resid = total[:, :rows], total[:, rows:]
    sum_sq = jnp.sum(resid * resid)
    sum_curv = jnp.sum(own_ref[rank:] * hess)
    lane = lax.broadcasted_iota(jnp.int32, inner_ref.shape, 1)
    inner_ref[...] = jnp.where(lane == 0, sum_sq, jnp.where(lane == 1, sum_curv, 0.0))


def out_kernel(total_ref, parts_ref, hess_ref, resid_ref, inner_ref):
    rows = hess_ref.shape[1]
    hess_ref[...] = total_ref[:, :rows]
    resid_ref[...] = total_ref[:, rows:]
    inner = jnp.sum(parts_ref[...], 0)
    for k in range(2):
        inner_ref[k] = jnp.sum(inner[:, k : k + 1])


def local(factors, tangent, counts):
    rank, rows = factors.shape
    nodes = counts.shape[1]
    blks, grps = lax.axis_size("blk"), lax.axis_size("grp")
    chips = grps // CORES
    vmem = pl.BlockSpec(memory_space=pltpu.VMEM)
    params = pltpu.CompilerParams(vmem_limit_bytes=40 * 1024 * 1024)

    def is_far():
        return lax.axis_index("grp") % CORES == FAR

    def call(kernel, name, out_shape, *args):
        return pl.pallas_call(
            kernel,
            out_shape=out_shape,
            in_specs=[vmem] * len(args),
            out_specs=jax.tree.map(lambda _: vmem, out_shape),
            compiler_params=params,
            name=name,
        )(*args)

    def shape(*dims, dtype=F32):
        return jax.ShapeDtypeStruct(dims, dtype)

    swap_cores = functools.partial(permute, blks=blks, chips=chips, moves=[(0, 0, 1)] * CORES)
    own = lax.optimization_barrier(jnp.concatenate([factors, tangent], 0))
    chip = jnp.concatenate([own, swap_cores(factors), swap_cores(tangent)], 0)
    (chip, counts) = lax.optimization_barrier((chip, counts))

    permutes, slots, groups = schedule(blks, chips)
    holds = {None: {FAR: (0, 0, FAR), NEAR: (0, 0, NEAR)}}
    for k, (src, *moves) in enumerate(permutes):
        sent = dict(zip((FAR, NEAR), moves))
        holds[k] = {}
        for core in (FAR, NEAR):
            sender = core ^ sent[core][2]
            b, x, first = holds[src][sender]
            holds[k][core] = (b ^ sent[sender][0], x ^ sent[sender][1], first)

    def places():
        b, g = lax.axis_index("blk"), lax.axis_index("grp")
        far, x = is_far(), g // CORES
        found = []
        for at_far, at_near in slots:
            ours, theirs = holds[at_far][FAR], holds[at_near][NEAR]
            step_b, step_x, first = (jnp.where(far, p, q) for p, q in zip(ours, theirs))
            found.append(((b ^ step_b) * chips + (x ^ step_x), first))
        return found

    *left, tiles = call(
        functools.partial(left_kernel, rank, places),
        "row_operands",
        (
            shape(4 * rows, 4 * rank, dtype=BF16),
            shape(4 * rows, 4 * rank, dtype=BF16),
            shape(2 * rows, 2 * rank, dtype=BF16),
            shape(len(slots), 2 * rows, 2 * rows),
        ),
        chip,
        counts,
        swap_cores(counts),
    )
    got = {None: chip}
    for k, (src, *moves) in enumerate(permutes):
        sent = dict(zip((FAR, NEAR), moves))
        if src is not None and permutes[k - 1][0] is None:
            (left, tiles, got[src]) = lax.optimization_barrier((left, tiles, got[src]))
        got[k] = permute(got[src], blks, chips, [sent[core] for core in range(CORES)])

    total = ()
    for group in groups:
        entries = [slots[k] for k in group]
        used = list(dict.fromkeys(k for entry in entries for k in entry))
        plan = [
            (used.index(p), used.index(q), FAR if p is None else NEAR if q is None else None)
            for p, q in entries
        ]
        part = group is groups[-1]
        total = call(
            functools.partial(chips_kernel, rank, is_far, plan, part, group[0]),
            "chips_%d" % group[0],
            (shape(rank, 2 * rows),) * 2 if part else (shape(rank, 4 * rows),),
            *left,
            tiles,
            *[got[k] for k in used],
            *total,
        )
    mine, theirs = total
    total, inner = call(
        functools.partial(finish_kernel, rank, 1.0 / nodes**0.5),
        "finish",
        (shape(rank, 2 * rows), shape(1, 128)),
        own,
        mine,
        swap_cores(theirs),
    )

    size = blks * grps
    parts = lax.all_to_all(
        jnp.broadcast_to(inner[None], (size, 1, 128)),
        AXES,
        0,
        0,
        axis_index_groups=[list(range(size))[::-1]],
        tiled=True,
    )
    return pl.pallas_call(
        out_kernel,
        out_shape=(shape(rank, rows), shape(rank, rows), shape(2)),
        in_specs=[vmem] * 2,
        out_specs=(vmem, vmem, pl.BlockSpec(memory_space=pltpu.SMEM)),
        name="results",
    )(*(pltpu.with_memory_space_constraint(a, pltpu.VMEM) for a in (total, parts)))


def solution(mesh):
    part = ("parts", "blk", "grp")
    return jax.shard_map(
        local,
        mesh=mesh,
        in_specs=(P(None, part), P(None, part), P(part, None)),
        out_specs=(P(None, part), P(None, part), P("parts")),
        check_vma=False,
    )
```

```python
import functools

import jax
import jax.numpy as jnp
from jax import lax
from jax.experimental import pallas as pl
from jax.experimental.pallas import tpu as pltpu
from jax.sharding import PartitionSpec as P

AXES = ("blk", "grp")
CORES = 2
FAR, NEAR = 1, 0
F32, BF16 = jnp.float32, jnp.bfloat16


def permute(x, blks, chips, moves):
    pairs = []
    for b in range(blks):
        for x_at in range(chips):
            for c in range(CORES):
                step = moves[c]
                to = ((b ^ step[0]) * chips + (x_at ^ step[1])) * CORES + (c ^ step[2])
                pairs.append(((b * chips + x_at) * CORES + c, to))
    return lax.ppermute(x, AXES, pairs)


def split2(x):
    hi = x.astype(BF16)
    return hi, (x - hi.astype(F32)).astype(BF16)


def split3(x):
    hi = x.astype(BF16)
    rest = x - hi.astype(F32)
    mid = rest.astype(BF16)
    return hi, mid, (rest - mid.astype(F32)).astype(BF16)


def dot(a, b):
    return lax.dot_general(a, b, (((1,), (0,)), ((), ())), preferred_element_type=F32)


def dot_t(a, b):
    return lax.dot_general(a, b, (((1,), (1,)), ((), ())), preferred_element_type=F32)


def schedule(blks, chips):
    half = blks // 2
    if (blks, chips) == (4, 2):
        ops = [
            (None, (2, 0, 0), (0, 1, 0)),
            (None, (3, 1, 1), (1, 0, 1)),
            (0, (1, 0, 1), (0, 0, 1)),
            (0, (0, 1, 1), (1, 0, 1)),
        ]
        return ops, [(None, 0), (0, 1), (1, 2), (3, 3)], [[0], [1], [2]]
    ops, slots = [], []
    far = [(b, x) for x in range(chips) for b in range(half, blks)]
    near = [(b, x) for x in range(chips) for b in range(half)][1:] + far[-1:]
    for k in range(len(far)):
        src = k % half if k >= half else None
        (fb, fx), (nb, nx) = (far[src], near[src]) if k >= half else ((0, 0), (0, 0))
        far_move = (far[k][0] ^ fb, far[k][1] ^ fx, 0)
        near_move = (near[k][0] ^ nb, near[k][1] ^ nx, 0)
        if k == len(far) - 1:
            far_move, near_move = (*far_move[:2], 1), (0, 0, 1)
        ops.append((src, far_move, near_move))
        slots.append((k, k))
    slots[-1] = (None, len(far) - 1)
    groups = [range(half), range(half, len(far) - 1)]
    return ops, slots, [group for group in groups if group]


def left_kernel(rank, places, chip_ref, counts_ref, other_ref, eta_ref, deta_ref, tiles_ref):
    span = 2 * rank
    nodes = jnp.concatenate([chip_ref[:span].T, chip_ref[span:].T], 0)
    uh, um, ul = split3(nodes[:, :rank])
    vh, vm = split2(nodes[:, rank:])
    eta_ref[...] = jnp.concatenate([uh, uh, um, um, ul, uh], 1)
    deta_ref[...] = jnp.concatenate([vh, vh, uh, uh, vm, vm, um, um], 1)
    for k, place in enumerate(places()):
        tiles_ref[k] = tile_of(counts_ref, other_ref, place).astype(F32)


def chip_terms(eta_left, deta_left, chip, counted, rank, diagonal, start=0):
    rows = eta_left.shape[0]
    span = 2 * rank
    cols = jnp.concatenate([chip[:span], chip[span:]], 1)
    uh, um, ul = split3(cols[:rank])
    vh, vm = split2(cols[rank:])
    eta = dot(eta_left, jnp.concatenate([uh, um, uh, um, uh, ul], 0))
    deta = dot(deta_left, jnp.concatenate([uh, um, vh, vm, uh, um, vh, vm], 0))
    rate = jnp.exp(eta)
    if diagonal is not None:
        at_row = start + lax.broadcasted_iota(jnp.int32, rate.shape, 0)
        at_col = lax.broadcasted_iota(jnp.int32, rate.shape, 1)
        keep = jnp.logical_or(at_row != at_col, jnp.logical_not(diagonal))
        rate = jnp.where(keep, rate, 0.0)
        counted = jnp.where(keep, counted, 0.0)
    weight = rate * deta
    wh, wm = split2(weight)
    sh, sm = split2(counted - rate - weight)
    out = dot_t(jnp.concatenate([uh, um], 0), jnp.concatenate([wh, sh, wm, sm], 0))
    total = out[:rank] + out[rank:]
    return total[:, : 2 * rows] + total[:, 2 * rows :]


def tile_of(counts_ref, other_counts_ref, place):
    rows = counts_ref.shape[0]
    chip, first = place
    lines = []
    for ref in (counts_ref, other_counts_ref):
        halves = [
            ref[:, pl.ds(pl.multiple_of((chip * CORES + half) * rows, rows), rows)]
            for half in (first, 1 - first)
        ]
        lines.append(jnp.concatenate(halves, 1))
    return jnp.concatenate(lines, 0)


def pick_chip(far, entry, blocks):
    at_far, at_near, own_core = entry
    chip = blocks[at_far][...]
    if at_far != at_near:
        chip = jnp.where(far, chip, blocks[at_near][...])
    return chip, {FAR: far, NEAR: jnp.logical_not(far), None: None}[own_core]


def chips_kernel(rank, is_far, plan, slot, count, *refs):
    eta_ref, deta_ref, tiles_ref = refs[:3]
    blocks, before = refs[3 : 3 + count], refs[3 + count : -1]
    far = is_far()
    total = before[0][...] if before else None
    for k, entry in enumerate(plan):
        chip, own = pick_chip(far, entry, blocks)
        terms = chip_terms(eta_ref[...], deta_ref[...], chip, tiles_ref[slot + k], rank, own)
        total = terms if total is None else total + terms
    refs[-1][...] = total


def last_kernel(rank, is_far, entry, slot, half, *refs):
    eta_ref, deta_ref, tiles_ref, *blocks, sum_ref, out_ref = refs
    rows = eta_ref.shape[0] // CORES
    mine = slice(half * rows, (half + 1) * rows)
    chip, own = pick_chip(is_far(), entry, blocks)
    terms = chip_terms(
        eta_ref[mine], deta_ref[mine], chip, tiles_ref[slot][mine], rank, own, half * rows
    )
    resid = slice((CORES + half) * rows, (CORES + half + 1) * rows)
    out_ref[...] = terms + jnp.concatenate([sum_ref[:, mine], sum_ref[:, resid]], 1)


def finish_kernel(rank, scale, own_ref, mine_ref, got_ref, total_ref, inner_ref):
    rows = own_ref.shape[1]
    total = (mine_ref[...] + got_ref[...]) * scale
    total_ref[...] = total
    hess, resid = total[:, :rows], total[:, rows:]
    sum_sq = jnp.sum(resid * resid)
    sum_curv = jnp.sum(own_ref[rank:] * hess)
    lane = lax.broadcasted_iota(jnp.int32, inner_ref.shape, 1)
    inner_ref[...] = jnp.where(lane == 0, sum_sq, jnp.where(lane == 1, sum_curv, 0.0))


def out_kernel(total_ref, parts_ref, hess_ref, resid_ref, inner_ref):
    rows = hess_ref.shape[1]
    hess_ref[...] = total_ref[:, :rows]
    resid_ref[...] = total_ref[:, rows:]
    inner = jnp.sum(parts_ref[...], 0)
    for k in range(2):
        inner_ref[k] = jnp.sum(inner[:, k : k + 1])


def local(factors, tangent, counts):
    rank, rows = factors.shape
    nodes = counts.shape[1]
    blks, grps = lax.axis_size("blk"), lax.axis_size("grp")
    chips = grps // CORES
    vmem = pl.BlockSpec(memory_space=pltpu.VMEM)
    params = pltpu.CompilerParams(vmem_limit_bytes=40 * 1024 * 1024)

    def is_far():
        return lax.axis_index("grp") % CORES == FAR

    def call(kernel, name, out_shape, *args):
        return pl.pallas_call(
            kernel,
            out_shape=out_shape,
            in_specs=[vmem] * len(args),
            out_specs=jax.tree.map(lambda _: vmem, out_shape),
            compiler_params=params,
            name=name,
        )(*args)

    def shape(*dims, dtype=F32):
        return jax.ShapeDtypeStruct(dims, dtype)

    swap_cores = functools.partial(permute, blks=blks, chips=chips, moves=[(0, 0, 1)] * CORES)
    own = lax.optimization_barrier(jnp.concatenate([factors, tangent], 0))
    chip = jnp.concatenate([own, swap_cores(factors), swap_cores(tangent)], 0)
    (chip, counts) = lax.optimization_barrier((chip, counts))

    permutes, slots, groups = schedule(blks, chips)
    holds = {None: {FAR: (0, 0, FAR), NEAR: (0, 0, NEAR)}}
    for k, (src, *moves) in enumerate(permutes):
        sent = dict(zip((FAR, NEAR), moves))
        holds[k] = {}
        for core in (FAR, NEAR):
            sender = core ^ sent[core][2]
            b, x, first = holds[src][sender]
            holds[k][core] = (b ^ sent[sender][0], x ^ sent[sender][1], first)

    def places():
        b, g = lax.axis_index("blk"), lax.axis_index("grp")
        far, x = is_far(), g // CORES
        found = []
        for at_far, at_near in slots:
            ours, theirs = holds[at_far][FAR], holds[at_near][NEAR]
            step_b, step_x, first = (jnp.where(far, p, q) for p, q in zip(ours, theirs))
            found.append(((b ^ step_b) * chips + (x ^ step_x), first))
        return found

    *left, tiles = call(
        functools.partial(left_kernel, rank, places),
        "row_operands",
        (
            shape(2 * rows, 6 * rank, dtype=BF16),
            shape(2 * rows, 8 * rank, dtype=BF16),
            shape(len(slots), 2 * rows, 2 * rows),
        ),
        chip,
        counts,
        swap_cores(counts),
    )
    got = {None: chip}
    for k, (src, *moves) in enumerate(permutes):
        sent = dict(zip((FAR, NEAR), moves))
        if src is not None and permutes[k - 1][0] is None:
            (left, tiles, got[src]) = lax.optimization_barrier((left, tiles, got[src]))
        got[k] = permute(got[src], blks, chips, [sent[core] for core in range(CORES)])

    def plan_of(entries):
        used = list(dict.fromkeys(k for entry in entries for k in entry))
        own = [FAR if p is None else NEAR if q is None else None for p, q in entries]
        plan = [(used.index(p), used.index(q), o) for (p, q), o in zip(entries, own)]
        return plan, [got[k] for k in used]

    total = ()
    for group in groups:
        plan, blocks = plan_of([slots[k] for k in group])
        total = call(
            functools.partial(chips_kernel, rank, is_far, plan, group[0], len(blocks)),
            "chips_%d" % group[0],
            (shape(rank, 4 * rows),),
            *left,
            tiles,
            *blocks,
            *total,
        )
    plan, blocks = plan_of(slots[-1:])
    theirs, mine = (
        call(
            functools.partial(last_kernel, rank, is_far, plan[0], len(slots) - 1, half),
            "last_chip_%d" % half,
            shape(rank, 2 * rows),
            *left,
            tiles,
            *blocks,
            *total,
        )
        for half in (1, 0)
    )
    total, inner = call(
        functools.partial(finish_kernel, rank, 1.0 / nodes**0.5),
        "finish",
        (shape(rank, 2 * rows), shape(1, 128)),
        own,
        mine,
        swap_cores(theirs),
    )

    size = blks * grps
    parts = lax.all_to_all(
        jnp.broadcast_to(inner[None], (size, 1, 128)),
        AXES,
        0,
        0,
        axis_index_groups=[list(range(size))[::-1]],
        tiled=True,
    )
    return pl.pallas_call(
        out_kernel,
        out_shape=(shape(rank, rows), shape(rank, rows), shape(2)),
        in_specs=[vmem] * 2,
        out_specs=(vmem, vmem, pl.BlockSpec(memory_space=pltpu.SMEM)),
        name="results",
    )(*(pltpu.with_memory_space_constraint(a, pltpu.VMEM) for a in (total, parts)))


def solution(mesh):
    part = ("parts", "blk", "grp")
    return jax.shard_map(
        local,
        mesh=mesh,
        in_specs=(P(None, part), P(None, part), P(part, None)),
        out_specs=(P(None, part), P(None, part), P("parts")),
        check_vma=False,
    )
```

```python
import functools

import jax
import jax.numpy as jnp
from jax import lax
from jax.experimental import pallas as pl
from jax.experimental.pallas import tpu as pltpu
from jax.sharding import PartitionSpec as P

AXES = ("blk", "grp")
CORES = 2
FAR, NEAR = 1, 0
F32, BF16 = jnp.float32, jnp.bfloat16


def permute(x, blks, chips, moves):
    pairs = []
    for b in range(blks):
        for x_at in range(chips):
            for c in range(CORES):
                step = moves[c]
                to = ((b ^ step[0]) * chips + (x_at ^ step[1])) * CORES + (c ^ step[2])
                pairs.append(((b * chips + x_at) * CORES + c, to))
    return lax.ppermute(x, AXES, pairs)


def split2(x):
    hi = x.astype(BF16)
    return hi, (x - hi.astype(F32)).astype(BF16)


def split3(x):
    hi = x.astype(BF16)
    rest = x - hi.astype(F32)
    mid = rest.astype(BF16)
    return hi, mid, (rest - mid.astype(F32)).astype(BF16)


def dot(a, b):
    return lax.dot_general(a, b, (((1,), (0,)), ((), ())), preferred_element_type=F32)


def dot_t(a, b):
    return lax.dot_general(a, b, (((1,), (1,)), ((), ())), preferred_element_type=F32)


def schedule(blks, chips):
    half = blks // 2
    if (blks, chips) == (4, 2):
        ops = [
            (None, (2, 0, 0), (0, 1, 0)),
            (None, (3, 1, 1), (1, 0, 1)),
            (0, (1, 0, 1), (0, 0, 1)),
            (0, (0, 1, 1), (1, 0, 1)),
        ]
        return ops, [(None, 0), (0, 1), (1, 2), (3, 3)], [[0], [1, 2]]
    ops, slots = [], []
    far = [(b, x) for x in range(chips) for b in range(half, blks)]
    near = [(b, x) for x in range(chips) for b in range(half)][1:] + far[-1:]
    for k in range(len(far)):
        src = k % half if k >= half else None
        (fb, fx), (nb, nx) = (far[src], near[src]) if k >= half else ((0, 0), (0, 0))
        far_move = (far[k][0] ^ fb, far[k][1] ^ fx, 0)
        near_move = (near[k][0] ^ nb, near[k][1] ^ nx, 0)
        if k == len(far) - 1:
            far_move, near_move = (*far_move[:2], 1), (0, 0, 1)
        ops.append((src, far_move, near_move))
        slots.append((k, k))
    slots[-1] = (None, len(far) - 1)
    groups = [range(half), range(half, len(far) - 1)]
    return ops, slots, [group for group in groups if group]


def left_kernel(rank, places, chip_ref, counts_ref, other_ref, eta_ref, deta_ref, tiles_ref):
    span = 2 * rank
    nodes = jnp.concatenate([chip_ref[:span].T, chip_ref[span:].T], 0)
    uh, um, ul = split3(nodes[:, :rank])
    vh, vm = split2(nodes[:, rank:])
    eta_ref[...] = jnp.concatenate([uh, uh, um, um, ul, uh], 1)
    deta_ref[...] = jnp.concatenate([vh, vh, uh, uh, vm, vm, um, um], 1)
    for k, place in enumerate(places()):
        tiles_ref[k] = tile_of(counts_ref, other_ref, place).astype(F32)


def chip_terms(eta_left, deta_left, chip, counted, rank, diagonal, start=0):
    rows = eta_left.shape[0]
    span = 2 * rank
    cols = jnp.concatenate([chip[:span], chip[span:]], 1)
    uh, um, ul = split3(cols[:rank])
    vh, vm = split2(cols[rank:])
    eta = dot(eta_left, jnp.concatenate([uh, um, uh, um, uh, ul], 0))
    deta = dot(deta_left, jnp.concatenate([uh, um, vh, vm, uh, um, vh, vm], 0))
    rate = jnp.exp(eta)
    if diagonal is not None:
        at_row = start + lax.broadcasted_iota(jnp.int32, rate.shape, 0)
        at_col = lax.broadcasted_iota(jnp.int32, rate.shape, 1)
        keep = jnp.logical_or(at_row != at_col, jnp.logical_not(diagonal))
        rate = jnp.where(keep, rate, 0.0)
        counted = jnp.where(keep, counted, 0.0)
    weight = rate * deta
    wh, wm = split2(weight)
    sh, sm = split2(counted - rate - weight)
    out = dot_t(jnp.concatenate([uh, um], 0), jnp.concatenate([wh, sh, wm, sm], 0))
    total = out[:rank] + out[rank:]
    return total[:, : 2 * rows] + total[:, 2 * rows :]


def tile_of(counts_ref, other_counts_ref, place):
    rows = counts_ref.shape[0]
    chip, first = place
    lines = []
    for ref in (counts_ref, other_counts_ref):
        halves = [
            ref[:, pl.ds(pl.multiple_of((chip * CORES + half) * rows, rows), rows)]
            for half in (first, 1 - first)
        ]
        lines.append(jnp.concatenate(halves, 1))
    return jnp.concatenate(lines, 0)


def pick_chip(far, entry, blocks):
    at_far, at_near, own_core = entry
    chip = blocks[at_far][...]
    if at_far != at_near:
        chip = jnp.where(far, chip, blocks[at_near][...])
    return chip, {FAR: far, NEAR: jnp.logical_not(far), None: None}[own_core]


def chips_kernel(rank, is_far, plan, slot, count, *refs):
    eta_ref, deta_ref, tiles_ref = refs[:3]
    blocks, before = refs[3 : 3 + count], refs[3 + count : -1]
    far = is_far()
    total = before[0][...] if before else None
    for k, entry in enumerate(plan):
        chip, own = pick_chip(far, entry, blocks)
        terms = chip_terms(eta_ref[...], deta_ref[...], chip, tiles_ref[slot + k], rank, own)
        total = terms if total is None else total + terms
    refs[-1][...] = total


def last_kernel(rank, is_far, entry, slot, half, *refs):
    eta_ref, deta_ref, tiles_ref, *blocks, sum_ref, out_ref = refs
    rows = eta_ref.shape[0] // CORES
    mine = slice(half * rows, (half + 1) * rows)
    chip, own = pick_chip(is_far(), entry, blocks)
    terms = chip_terms(
        eta_ref[mine], deta_ref[mine], chip, tiles_ref[slot][mine], rank, own, half * rows
    )
    resid = slice((CORES + half) * rows, (CORES + half + 1) * rows)
    out_ref[...] = terms + jnp.concatenate([sum_ref[:, mine], sum_ref[:, resid]], 1)


def finish_kernel(rank, scale, own_ref, mine_ref, got_ref, total_ref, inner_ref):
    rows = own_ref.shape[1]
    total = (mine_ref[...] + got_ref[...]) * scale
    total_ref[...] = total
    hess, resid = total[:, :rows], total[:, rows:]
    sum_sq = jnp.sum(resid * resid)
    sum_curv = jnp.sum(own_ref[rank:] * hess)
    lane = lax.broadcasted_iota(jnp.int32, inner_ref.shape, 1)
    inner_ref[...] = jnp.where(lane == 0, sum_sq, jnp.where(lane == 1, sum_curv, 0.0))


def out_kernel(total_ref, parts_ref, hess_ref, resid_ref, inner_ref):
    rows = hess_ref.shape[1]
    hess_ref[...] = total_ref[:, :rows]
    resid_ref[...] = total_ref[:, rows:]
    inner = jnp.sum(parts_ref[...], 0)
    for k in range(2):
        inner_ref[k] = jnp.sum(inner[:, k : k + 1])


def local(factors, tangent, counts):
    rank, rows = factors.shape
    nodes = counts.shape[1]
    blks, grps = lax.axis_size("blk"), lax.axis_size("grp")
    chips = grps // CORES
    vmem = pl.BlockSpec(memory_space=pltpu.VMEM)
    params = pltpu.CompilerParams(vmem_limit_bytes=40 * 1024 * 1024)

    def is_far():
        return lax.axis_index("grp") % CORES == FAR

    def call(kernel, name, out_shape, *args):
        return pl.pallas_call(
            kernel,
            out_shape=out_shape,
            in_specs=[vmem] * len(args),
            out_specs=jax.tree.map(lambda _: vmem, out_shape),
            compiler_params=params,
            name=name,
        )(*args)

    def shape(*dims, dtype=F32):
        return jax.ShapeDtypeStruct(dims, dtype)

    swap_cores = functools.partial(permute, blks=blks, chips=chips, moves=[(0, 0, 1)] * CORES)
    own = lax.optimization_barrier(jnp.concatenate([factors, tangent], 0))
    chip = jnp.concatenate([own, swap_cores(factors), swap_cores(tangent)], 0)
    (chip, counts) = lax.optimization_barrier((chip, counts))

    permutes, slots, groups = schedule(blks, chips)
    holds = {None: {FAR: (0, 0, FAR), NEAR: (0, 0, NEAR)}}
    for k, (src, *moves) in enumerate(permutes):
        sent = dict(zip((FAR, NEAR), moves))
        holds[k] = {}
        for core in (FAR, NEAR):
            sender = core ^ sent[core][2]
            b, x, first = holds[src][sender]
            holds[k][core] = (b ^ sent[sender][0], x ^ sent[sender][1], first)

    def places():
        b, g = lax.axis_index("blk"), lax.axis_index("grp")
        far, x = is_far(), g // CORES
        found = []
        for at_far, at_near in slots:
            ours, theirs = holds[at_far][FAR], holds[at_near][NEAR]
            step_b, step_x, first = (jnp.where(far, p, q) for p, q in zip(ours, theirs))
            found.append(((b ^ step_b) * chips + (x ^ step_x), first))
        return found

    *left, tiles = call(
        functools.partial(left_kernel, rank, places),
        "row_operands",
        (
            shape(2 * rows, 6 * rank, dtype=BF16),
            shape(2 * rows, 8 * rank, dtype=BF16),
            shape(len(slots), 2 * rows, 2 * rows),
        ),
        chip,
        counts,
        swap_cores(counts),
    )
    got = {None: chip}
    for k, (src, *moves) in enumerate(permutes):
        sent = dict(zip((FAR, NEAR), moves))
        if src is not None and permutes[k - 1][0] is None:
            (left, tiles, got[src]) = lax.optimization_barrier((left, tiles, got[src]))
        got[k] = permute(got[src], blks, chips, [sent[core] for core in range(CORES)])

    def plan_of(entries):
        used = list(dict.fromkeys(k for entry in entries for k in entry))
        own = [FAR if p is None else NEAR if q is None else None for p, q in entries]
        plan = [(used.index(p), used.index(q), o) for (p, q), o in zip(entries, own)]
        return plan, [got[k] for k in used]

    total = ()
    for group in groups:
        plan, blocks = plan_of([slots[k] for k in group])
        total = call(
            functools.partial(chips_kernel, rank, is_far, plan, group[0], len(blocks)),
            "chips_%d" % group[0],
            (shape(rank, 4 * rows),),
            *left,
            tiles,
            *blocks,
            *total,
        )
    plan, blocks = plan_of(slots[-1:])
    theirs, mine = (
        call(
            functools.partial(last_kernel, rank, is_far, plan[0], len(slots) - 1, half),
            "last_chip_%d" % half,
            shape(rank, 2 * rows),
            *left,
            tiles,
            *blocks,
            *total,
        )
        for half in (1, 0)
    )
    total, inner = call(
        functools.partial(finish_kernel, rank, 1.0 / nodes**0.5),
        "finish",
        (shape(rank, 2 * rows), shape(1, 128)),
        own,
        mine,
        swap_cores(theirs),
    )

    size = blks * grps
    parts = lax.all_to_all(
        pltpu.with_memory_space_constraint(
            jnp.broadcast_to(inner[None], (size, 1, 128)), pltpu.VMEM
        ),
        AXES,
        0,
        0,
        axis_index_groups=[list(range(size))[::-1]],
        tiled=True,
    )
    return pl.pallas_call(
        out_kernel,
        out_shape=(shape(rank, rows), shape(rank, rows), shape(2)),
        in_specs=[vmem] * 2,
        out_specs=(vmem, vmem, pl.BlockSpec(memory_space=pltpu.SMEM)),
        name="results",
    )(*(pltpu.with_memory_space_constraint(a, pltpu.VMEM) for a in (total, parts)))


def solution(mesh):
    part = ("parts", "blk", "grp")
    return jax.shard_map(
        local,
        mesh=mesh,
        in_specs=(P(None, part), P(None, part), P(part, None)),
        out_specs=(P(None, part), P(None, part), P("parts")),
        check_vma=False,
    )
```

```python
import functools

import jax
import jax.numpy as jnp
from jax import lax
from jax.experimental import pallas as pl
from jax.experimental.pallas import tpu as pltpu
from jax.sharding import PartitionSpec as P

AXES = ("blk", "grp")
CORES = 2
FAR, NEAR = 1, 0
F32, BF16 = jnp.float32, jnp.bfloat16


def permute(x, blks, chips, moves):
    pairs = []
    for b in range(blks):
        for x_at in range(chips):
            for c in range(CORES):
                step = moves[c]
                to = ((b ^ step[0]) * chips + (x_at ^ step[1])) * CORES + (c ^ step[2])
                pairs.append(((b * chips + x_at) * CORES + c, to))
    return lax.ppermute(x, AXES, pairs)


def split2(x):
    hi = x.astype(BF16)
    return hi, (x - hi.astype(F32)).astype(BF16)


def split3(x):
    hi = x.astype(BF16)
    rest = x - hi.astype(F32)
    mid = rest.astype(BF16)
    return hi, mid, (rest - mid.astype(F32)).astype(BF16)


def dot(a, b):
    return lax.dot_general(a, b, (((1,), (0,)), ((), ())), preferred_element_type=F32)


def dot_t(a, b):
    return lax.dot_general(a, b, (((1,), (1,)), ((), ())), preferred_element_type=F32)


def schedule(blks, chips):
    half = blks // 2
    if (blks, chips) == (4, 2):
        ops = [
            (None, (2, 0, 0), (0, 1, 0)),
            (None, (3, 1, 1), (1, 0, 1)),
            (0, (1, 0, 1), (0, 0, 1)),
            (0, (0, 1, 1), (1, 0, 1)),
        ]
        return ops, [(None, 0), (0, 1), (1, 2), (3, 3)], [[0], [1], [2]]
    ops, slots = [], []
    far = [(b, x) for x in range(chips) for b in range(half, blks)]
    near = [(b, x) for x in range(chips) for b in range(half)][1:] + far[-1:]
    for k in range(len(far)):
        src = k % half if k >= half else None
        (fb, fx), (nb, nx) = (far[src], near[src]) if k >= half else ((0, 0), (0, 0))
        far_move = (far[k][0] ^ fb, far[k][1] ^ fx, 0)
        near_move = (near[k][0] ^ nb, near[k][1] ^ nx, 0)
        if k == len(far) - 1:
            far_move, near_move = (*far_move[:2], 1), (0, 0, 1)
        ops.append((src, far_move, near_move))
        slots.append((k, k))
    slots[-1] = (None, len(far) - 1)
    groups = [range(half), range(half, len(far) - 1)]
    return ops, slots, [group for group in groups if group]


def left_kernel(rank, places, chip_ref, counts_ref, other_ref, eta_ref, deta_ref, tiles_ref):
    span = 2 * rank
    nodes = jnp.concatenate([chip_ref[:span].T, chip_ref[span:].T], 0)
    uh, um, ul = split3(nodes[:, :rank])
    vh, vm = split2(nodes[:, rank:])
    eta_ref[...] = jnp.concatenate([uh, uh, um, um, ul, uh], 1)
    deta_ref[...] = jnp.concatenate([vh, vh, uh, uh, vm, vm, um, um], 1)
    for k, place in enumerate(places()):
        tiles_ref[k] = tile_of(counts_ref, other_ref, place).astype(F32)


def chip_terms(eta_left, deta_left, chip, counted, rank, diagonal, start=0):
    rows = eta_left.shape[0]
    span = 2 * rank
    cols = jnp.concatenate([chip[:span], chip[span:]], 1)
    uh, um, ul = split3(cols[:rank])
    vh, vm = split2(cols[rank:])
    eta = dot(eta_left, jnp.concatenate([uh, um, uh, um, uh, ul], 0))
    deta = dot(deta_left, jnp.concatenate([uh, um, vh, vm, uh, um, vh, vm], 0))
    rate = jnp.exp(eta)
    if diagonal is not None:
        at_row = start + lax.broadcasted_iota(jnp.int32, rate.shape, 0)
        at_col = lax.broadcasted_iota(jnp.int32, rate.shape, 1)
        keep = jnp.logical_or(at_row != at_col, jnp.logical_not(diagonal))
        rate = jnp.where(keep, rate, 0.0)
        counted = jnp.where(keep, counted, 0.0)
    weight = rate * deta
    wh, wm = split2(weight)
    sh, sm = split2(counted - rate - weight)
    out = dot_t(jnp.concatenate([uh, um], 0), jnp.concatenate([wh, sh, wm, sm], 0))
    total = out[:rank] + out[rank:]
    return total[:, : 2 * rows] + total[:, 2 * rows :]


def tile_of(counts_ref, other_counts_ref, place):
    rows = counts_ref.shape[0]
    chip, first = place
    lines = []
    for ref in (counts_ref, other_counts_ref):
        halves = [
            ref[:, pl.ds(pl.multiple_of((chip * CORES + half) * rows, rows), rows)]
            for half in (first, 1 - first)
        ]
        lines.append(jnp.concatenate(halves, 1))
    return jnp.concatenate(lines, 0)


def pick_chip(far, entry, blocks):
    at_far, at_near, own_core = entry
    chip = blocks[at_far][...]
    if at_far != at_near:
        chip = jnp.where(far, chip, blocks[at_near][...])
    return chip, {FAR: far, NEAR: jnp.logical_not(far), None: None}[own_core]


def chips_kernel(rank, is_far, plan, slot, count, *refs):
    eta_ref, deta_ref, tiles_ref = refs[:3]
    blocks, before = refs[3 : 3 + count], refs[3 + count : -1]
    far = is_far()
    total = before[0][...] if before else None
    for k, entry in enumerate(plan):
        chip, own = pick_chip(far, entry, blocks)
        terms = chip_terms(eta_ref[...], deta_ref[...], chip, tiles_ref[slot + k], rank, own)
        total = terms if total is None else total + terms
    refs[-1][...] = total


def last_kernel(rank, is_far, entry, slot, half, *refs):
    eta_ref, deta_ref, tiles_ref, *blocks, sum_ref, out_ref = refs
    rows = eta_ref.shape[0] // CORES
    mine = slice(half * rows, (half + 1) * rows)
    chip, own = pick_chip(is_far(), entry, blocks)
    terms = chip_terms(
        eta_ref[mine], deta_ref[mine], chip, tiles_ref[slot][mine], rank, own, half * rows
    )
    resid = slice((CORES + half) * rows, (CORES + half + 1) * rows)
    out_ref[...] = terms + jnp.concatenate([sum_ref[:, mine], sum_ref[:, resid]], 1)


def finish_kernel(rank, scale, own_ref, mine_ref, got_ref, total_ref, inner_ref):
    rows = own_ref.shape[1]
    total = (mine_ref[...] + got_ref[...]) * scale
    total_ref[...] = total
    hess, resid = total[:, :rows], total[:, rows:]
    sum_sq = jnp.sum(resid * resid)
    sum_curv = jnp.sum(own_ref[rank:] * hess)
    lane = lax.broadcasted_iota(jnp.int32, inner_ref.shape, 1)
    inner_ref[...] = jnp.where(lane == 0, sum_sq, jnp.where(lane == 1, sum_curv, 0.0))


def out_kernel(total_ref, parts_ref, hess_ref, resid_ref, inner_ref):
    rows = hess_ref.shape[1]
    hess_ref[...] = total_ref[:, :rows]
    resid_ref[...] = total_ref[:, rows:]
    inner = jnp.sum(parts_ref[...], 0)
    for k in range(2):
        inner_ref[k] = jnp.sum(inner[:, k : k + 1])


def local(factors, tangent, counts):
    rank, rows = factors.shape
    nodes = counts.shape[1]
    blks, grps = lax.axis_size("blk"), lax.axis_size("grp")
    chips = grps // CORES
    vmem = pl.BlockSpec(memory_space=pltpu.VMEM)
    params = pltpu.CompilerParams(vmem_limit_bytes=40 * 1024 * 1024)

    def is_far():
        return lax.axis_index("grp") % CORES == FAR

    def call(kernel, name, out_shape, *args):
        return pl.pallas_call(
            kernel,
            out_shape=out_shape,
            in_specs=[vmem] * len(args),
            out_specs=jax.tree.map(lambda _: vmem, out_shape),
            compiler_params=params,
            name=name,
        )(*args)

    def shape(*dims, dtype=F32):
        return jax.ShapeDtypeStruct(dims, dtype)

    swap_cores = functools.partial(permute, blks=blks, chips=chips, moves=[(0, 0, 1)] * CORES)
    own = lax.optimization_barrier(jnp.concatenate([factors, tangent], 0))
    chip = jnp.concatenate([own, swap_cores(factors), swap_cores(tangent)], 0)
    (chip, counts) = lax.optimization_barrier((chip, counts))

    permutes, slots, groups = schedule(blks, chips)
    holds = {None: {FAR: (0, 0, FAR), NEAR: (0, 0, NEAR)}}
    for k, (src, *moves) in enumerate(permutes):
        sent = dict(zip((FAR, NEAR), moves))
        holds[k] = {}
        for core in (FAR, NEAR):
            sender = core ^ sent[core][2]
            b, x, first = holds[src][sender]
            holds[k][core] = (b ^ sent[sender][0], x ^ sent[sender][1], first)

    def places():
        b, g = lax.axis_index("blk"), lax.axis_index("grp")
        far, x = is_far(), g // CORES
        found = []
        for at_far, at_near in slots:
            ours, theirs = holds[at_far][FAR], holds[at_near][NEAR]
            step_b, step_x, first = (jnp.where(far, p, q) for p, q in zip(ours, theirs))
            found.append(((b ^ step_b) * chips + (x ^ step_x), first))
        return found

    *left, tiles = call(
        functools.partial(left_kernel, rank, places),
        "row_operands",
        (
            shape(2 * rows, 6 * rank, dtype=BF16),
            shape(2 * rows, 8 * rank, dtype=BF16),
            shape(len(slots), 2 * rows, 2 * rows),
        ),
        chip,
        counts,
        swap_cores(counts),
    )
    got = {None: chip}
    for k, (src, *moves) in enumerate(permutes):
        sent = dict(zip((FAR, NEAR), moves))
        if src is not None and permutes[k - 1][0] is None:
            (left, tiles, got[src]) = lax.optimization_barrier((left, tiles, got[src]))
        got[k] = permute(got[src], blks, chips, [sent[core] for core in range(CORES)])

    def plan_of(entries):
        used = list(dict.fromkeys(k for entry in entries for k in entry))
        own = [FAR if p is None else NEAR if q is None else None for p, q in entries]
        plan = [(used.index(p), used.index(q), o) for (p, q), o in zip(entries, own)]
        return plan, [got[k] for k in used]

    total = ()
    for group in groups:
        plan, blocks = plan_of([slots[k] for k in group])
        total = call(
            functools.partial(chips_kernel, rank, is_far, plan, group[0], len(blocks)),
            "chips_%d" % group[0],
            (shape(rank, 4 * rows),),
            *left,
            tiles,
            *blocks,
            *total,
        )
    plan, blocks = plan_of(slots[-1:])
    theirs, mine = (
        call(
            functools.partial(last_kernel, rank, is_far, plan[0], len(slots) - 1, half),
            "last_chip_%d" % half,
            shape(rank, 2 * rows),
            *left,
            tiles,
            *blocks,
            *total,
        )
        for half in (1, 0)
    )
    total, inner = call(
        functools.partial(finish_kernel, rank, 1.0 / nodes**0.5),
        "finish",
        (shape(rank, 2 * rows), shape(1, 128)),
        own,
        mine,
        swap_cores(theirs),
    )

    size = blks * grps
    parts = lax.all_to_all(
        jnp.broadcast_to(inner[None], (size, 1, 128)),
        AXES,
        0,
        0,
        axis_index_groups=[[size - 1, *range(size - 1)]],
        tiled=True,
    )
    return pl.pallas_call(
        out_kernel,
        out_shape=(shape(rank, rows), shape(rank, rows), shape(2)),
        in_specs=[vmem] * 2,
        out_specs=(vmem, vmem, pl.BlockSpec(memory_space=pltpu.SMEM)),
        name="results",
    )(*(pltpu.with_memory_space_constraint(a, pltpu.VMEM) for a in (total, parts)))


def solution(mesh):
    part = ("parts", "blk", "grp")
    return jax.shard_map(
        local,
        mesh=mesh,
        in_specs=(P(None, part), P(None, part), P(part, None)),
        out_specs=(P(None, part), P(None, part), P("parts")),
        check_vma=False,
    )
```

```python
import functools

import jax
import jax.numpy as jnp
from jax import lax
from jax.experimental import pallas as pl
from jax.experimental.pallas import tpu as pltpu
from jax.sharding import PartitionSpec as P

AXES = ("blk", "grp")
CORES = 2
FAR, NEAR = 1, 0
F32, BF16 = jnp.float32, jnp.bfloat16


def permute(x, blks, chips, moves):
    pairs = []
    for b in range(blks):
        for x_at in range(chips):
            for c in range(CORES):
                step = moves[c]
                to = ((b ^ step[0]) * chips + (x_at ^ step[1])) * CORES + (c ^ step[2])
                pairs.append(((b * chips + x_at) * CORES + c, to))
    return lax.ppermute(x, AXES, pairs)


def split2(x):
    hi = x.astype(BF16)
    return hi, (x - hi.astype(F32)).astype(BF16)


def split3(x):
    hi = x.astype(BF16)
    rest = x - hi.astype(F32)
    mid = rest.astype(BF16)
    return hi, mid, (rest - mid.astype(F32)).astype(BF16)


def dot(a, b):
    return lax.dot_general(a, b, (((1,), (0,)), ((), ())), preferred_element_type=F32)


def dot_t(a, b):
    return lax.dot_general(a, b, (((1,), (1,)), ((), ())), preferred_element_type=F32)


def schedule(blks, chips):
    half = blks // 2
    if (blks, chips) == (4, 2):
        ops = [
            (None, (2, 0, 0), (0, 1, 0)),
            (None, (3, 1, 1), (1, 0, 1)),
            (0, (1, 0, 1), (0, 0, 1)),
            (0, (0, 1, 1), (1, 0, 1)),
        ]
        return ops, [(None, 0), (0, 1), (1, 2), (3, 3)], [[0], [1], [2]]
    ops, slots = [], []
    far = [(b, x) for x in range(chips) for b in range(half, blks)]
    near = [(b, x) for x in range(chips) for b in range(half)][1:] + far[-1:]
    for k in range(len(far)):
        src = k % half if k >= half else None
        (fb, fx), (nb, nx) = (far[src], near[src]) if k >= half else ((0, 0), (0, 0))
        far_move = (far[k][0] ^ fb, far[k][1] ^ fx, 0)
        near_move = (near[k][0] ^ nb, near[k][1] ^ nx, 0)
        if k == len(far) - 1:
            far_move, near_move = (*far_move[:2], 1), (0, 0, 1)
        ops.append((src, far_move, near_move))
        slots.append((k, k))
    slots[-1] = (None, len(far) - 1)
    groups = [range(half), range(half, len(far) - 1)]
    return ops, slots, [group for group in groups if group]


def left_kernel(rank, places, chip_ref, counts_ref, other_ref, eta_ref, deta_ref, tiles_ref):
    span = 2 * rank
    nodes = jnp.concatenate([chip_ref[:span].T, chip_ref[span:].T], 0)
    uh, um, ul = split3(nodes[:, :rank])
    vh, vm = split2(nodes[:, rank:])
    eta_ref[...] = jnp.concatenate([uh, uh, um, um, ul, uh], 1)
    deta_ref[...] = jnp.concatenate([vh, vh, uh, uh, vm, vm, um, um], 1)
    for k, place in enumerate(places()):
        tiles_ref[k] = tile_of(counts_ref, other_ref, place).astype(F32)


def chip_terms(eta_left, deta_left, chip, counted, rank, diagonal, start=0):
    rows = eta_left.shape[0]
    span = 2 * rank
    cols = jnp.concatenate([chip[:span], chip[span:]], 1)
    uh, um, ul = split3(cols[:rank])
    vh, vm = split2(cols[rank:])
    eta = dot(eta_left, jnp.concatenate([uh, um, uh, um, uh, ul], 0))
    deta = dot(deta_left, jnp.concatenate([uh, um, vh, vm, uh, um, vh, vm], 0))
    rate = jnp.exp(eta)
    if diagonal is not None:
        at_row = start + lax.broadcasted_iota(jnp.int32, rate.shape, 0)
        at_col = lax.broadcasted_iota(jnp.int32, rate.shape, 1)
        keep = jnp.logical_or(at_row != at_col, jnp.logical_not(diagonal))
        rate = jnp.where(keep, rate, 0.0)
        counted = jnp.where(keep, counted, 0.0)
    weight = rate * deta
    wh, wm = split2(weight)
    sh, sm = split2(counted - rate - weight)
    out = dot_t(jnp.concatenate([uh, um], 0), jnp.concatenate([wh, sh, wm, sm], 0))
    total = out[:rank] + out[rank:]
    return total[:, : 2 * rows] + total[:, 2 * rows :]


def tile_of(counts_ref, other_counts_ref, place):
    rows = counts_ref.shape[0]
    chip, first = place
    lines = []
    for ref in (counts_ref, other_counts_ref):
        halves = [
            ref[:, pl.ds(pl.multiple_of((chip * CORES + half) * rows, rows), rows)]
            for half in (first, 1 - first)
        ]
        lines.append(jnp.concatenate(halves, 1))
    return jnp.concatenate(lines, 0)


def pick_chip(far, entry, blocks):
    at_far, at_near, own_core = entry
    chip = blocks[at_far][...]
    if at_far != at_near:
        chip = jnp.where(far, chip, blocks[at_near][...])
    return chip, {FAR: far, NEAR: jnp.logical_not(far), None: None}[own_core]


def chips_kernel(rank, is_far, plan, slot, count, *refs):
    eta_ref, deta_ref, tiles_ref = refs[:3]
    blocks, before = refs[3 : 3 + count], refs[3 + count : -1]
    far = is_far()
    total = before[0][...] if before else None
    for k, entry in enumerate(plan):
        chip, own = pick_chip(far, entry, blocks)
        terms = chip_terms(eta_ref[...], deta_ref[...], chip, tiles_ref[slot + k], rank, own)
        total = terms if total is None else total + terms
    refs[-1][...] = total


def last_kernel(rank, is_far, entry, slot, half, *refs):
    eta_ref, deta_ref, tiles_ref, *blocks, sum_ref, out_ref = refs
    rows = eta_ref.shape[0] // CORES
    mine = slice(half * rows, (half + 1) * rows)
    chip, own = pick_chip(is_far(), entry, blocks)
    terms = chip_terms(
        eta_ref[mine], deta_ref[mine], chip, tiles_ref[slot][mine], rank, own, half * rows
    )
    resid = slice((CORES + half) * rows, (CORES + half + 1) * rows)
    out_ref[...] = terms + jnp.concatenate([sum_ref[:, mine], sum_ref[:, resid]], 1)


def finish_kernel(rank, scale, own_ref, mine_ref, got_ref, total_ref, inner_ref):
    rows = own_ref.shape[1]
    total = (mine_ref[...] + got_ref[...]) * scale
    total_ref[...] = total
    hess, resid = total[:, :rows], total[:, rows:]
    sum_sq = jnp.sum(resid * resid)
    sum_curv = jnp.sum(own_ref[rank:] * hess)
    lane = lax.broadcasted_iota(jnp.int32, inner_ref.shape, 1)
    inner_ref[...] = jnp.where(lane == 0, sum_sq, jnp.where(lane == 1, sum_curv, 0.0))


def out_kernel(total_ref, parts_ref, hess_ref, resid_ref, inner_ref):
    rows = hess_ref.shape[1]
    hess_ref[...] = total_ref[:, :rows]
    resid_ref[...] = total_ref[:, rows:]
    inner = jnp.sum(parts_ref[...], 0)
    for k in range(2):
        inner_ref[k] = jnp.sum(inner[:, k : k + 1])


def local(factors, tangent, counts):
    rank, rows = factors.shape
    nodes = counts.shape[1]
    blks, grps = lax.axis_size("blk"), lax.axis_size("grp")
    chips = grps // CORES
    vmem = pl.BlockSpec(memory_space=pltpu.VMEM)
    params = pltpu.CompilerParams(vmem_limit_bytes=16 * 1024 * 1024)

    def is_far():
        return lax.axis_index("grp") % CORES == FAR

    def call(kernel, name, out_shape, *args):
        return pl.pallas_call(
            kernel,
            out_shape=out_shape,
            in_specs=[vmem] * len(args),
            out_specs=jax.tree.map(lambda _: vmem, out_shape),
            compiler_params=params,
            name=name,
        )(*args)

    def shape(*dims, dtype=F32):
        return jax.ShapeDtypeStruct(dims, dtype)

    swap_cores = functools.partial(permute, blks=blks, chips=chips, moves=[(0, 0, 1)] * CORES)
    own = lax.optimization_barrier(jnp.concatenate([factors, tangent], 0))
    chip = jnp.concatenate([own, swap_cores(factors), swap_cores(tangent)], 0)
    (chip, counts) = lax.optimization_barrier((chip, counts))

    permutes, slots, groups = schedule(blks, chips)
    holds = {None: {FAR: (0, 0, FAR), NEAR: (0, 0, NEAR)}}
    for k, (src, *moves) in enumerate(permutes):
        sent = dict(zip((FAR, NEAR), moves))
        holds[k] = {}
        for core in (FAR, NEAR):
            sender = core ^ sent[core][2]
            b, x, first = holds[src][sender]
            holds[k][core] = (b ^ sent[sender][0], x ^ sent[sender][1], first)

    def places():
        b, g = lax.axis_index("blk"), lax.axis_index("grp")
        far, x = is_far(), g // CORES
        found = []
        for at_far, at_near in slots:
            ours, theirs = holds[at_far][FAR], holds[at_near][NEAR]
            step_b, step_x, first = (jnp.where(far, p, q) for p, q in zip(ours, theirs))
            found.append(((b ^ step_b) * chips + (x ^ step_x), first))
        return found

    *left, tiles = call(
        functools.partial(left_kernel, rank, places),
        "row_operands",
        (
            shape(2 * rows, 6 * rank, dtype=BF16),
            shape(2 * rows, 8 * rank, dtype=BF16),
            shape(len(slots), 2 * rows, 2 * rows),
        ),
        chip,
        counts,
        swap_cores(counts),
    )
    got = {None: chip}
    for k, (src, *moves) in enumerate(permutes):
        sent = dict(zip((FAR, NEAR), moves))
        if src is not None and permutes[k - 1][0] is None:
            (left, tiles, got[src]) = lax.optimization_barrier((left, tiles, got[src]))
        got[k] = permute(got[src], blks, chips, [sent[core] for core in range(CORES)])

    def plan_of(entries):
        used = list(dict.fromkeys(k for entry in entries for k in entry))
        own = [FAR if p is None else NEAR if q is None else None for p, q in entries]
        plan = [(used.index(p), used.index(q), o) for (p, q), o in zip(entries, own)]
        return plan, [got[k] for k in used]

    total = ()
    for group in groups:
        plan, blocks = plan_of([slots[k] for k in group])
        total = call(
            functools.partial(chips_kernel, rank, is_far, plan, group[0], len(blocks)),
            "chips_%d" % group[0],
            (shape(rank, 4 * rows),),
            *left,
            tiles,
            *blocks,
            *total,
        )
    plan, blocks = plan_of(slots[-1:])
    theirs, mine = (
        call(
            functools.partial(last_kernel, rank, is_far, plan[0], len(slots) - 1, half),
            "last_chip_%d" % half,
            shape(rank, 2 * rows),
            *left,
            tiles,
            *blocks,
            *total,
        )
        for half in (1, 0)
    )
    total, inner = call(
        functools.partial(finish_kernel, rank, 1.0 / nodes**0.5),
        "finish",
        (shape(rank, 2 * rows), shape(1, 128)),
        own,
        mine,
        swap_cores(theirs),
    )

    size = blks * grps
    parts = lax.all_to_all(
        jnp.broadcast_to(inner[None], (size, 1, 128)),
        AXES,
        0,
        0,
        axis_index_groups=[[size - 1, *range(size - 1)]],
        tiled=True,
    )
    return pl.pallas_call(
        out_kernel,
        out_shape=(shape(rank, rows), shape(rank, rows), shape(2)),
        in_specs=[vmem] * 2,
        out_specs=(vmem, vmem, pl.BlockSpec(memory_space=pltpu.SMEM)),
        name="results",
    )(*(pltpu.with_memory_space_constraint(a, pltpu.VMEM) for a in (total, parts)))


def solution(mesh):
    part = ("parts", "blk", "grp")
    return jax.shard_map(
        local,
        mesh=mesh,
        in_specs=(P(None, part), P(None, part), P(part, None)),
        out_specs=(P(None, part), P(None, part), P("parts")),
        check_vma=False,
    )
```
